256 devices in a mesh: rep: 4 (over y), fsdp: 16 (over z, x_hi), tp: 4 (over x_lo, core).
Axes of the slice: x: 4 (x_hi: 2, x_lo: 2; x = x_hi * 2 + x_lo), y: 4, z: 8, core: 2. Of those that a mesh axis runs over, the one named last changes fastest.
Arguments:
- grad_parts: bfloat16 [4, 32, 4096, 1536], P('rep', None, 'fsdp', 'tp'), may hold values from -3 to 3
- momentum: bfloat16 [32, 4096, 1536], P('rep', 'fsdp', 'tp'), may hold values from -40 to 40
- basis: bfloat16 [32, 1536, 256], P('rep', 'tp'), may hold values from -0.15625 to 0.15625
Outputs:
- momentum_next: bfloat16 [32, 4096, 1536], P('rep', 'fsdp', 'tp')
- basis_next: bfloat16 [32, 1536, 256], P('rep', 'tp')
- update: bfloat16 [32, 4096, 1536], P('rep', 'fsdp', 'tp')
The draws below stay inside these ranges and needn't reach their ends.
All inputs are finite; a program needn't handle non-finite values.
Results may differ from the reference program's by a relative error of at most 0.023.
Values may be sent and summed in bfloat16 or wider, within the bound.
A program may use at most 64 MiB of HBM per device.

```python
import math
import jax
import jax.numpy as jnp
from jax import lax

D = 4096
FF = 1536
RANK = 256
EXPERTS = 32
N_REP = 4


def column_scales(key, slope):
    position = jnp.arange(FF, dtype=jnp.float32) / FF
    ramp = jnp.exp(math.log(10.0) * (slope * position - 0.6))
    rough = jnp.exp(jax.random.uniform(key, (EXPERTS, 1, FF), jnp.float32, math.log(0.7), math.log(1.4)))
    return ramp[None, None, :] * rough


def draw_momentum(key, part):
    key = jax.random.fold_in(key, 11)
    key_base, key_rows, key_cols = jax.random.split(key, 3)
    shape = (EXPERTS, D, FF)
    base = jax.random.truncated_normal(key_base, -4.0, 4.0, shape, jnp.float32)
    col_scale = column_scales(key_cols, 0.8)
    row_scale = jnp.exp(jax.random.uniform(key_rows, (EXPERTS, D, 1), jnp.float32, 0.0, math.log(10.0))) / math.sqrt(10.0)
    return (base * row_scale * col_scale).astype(jnp.bfloat16)


def raised(array, stream_key, source, target, blocks, factor):
    def block_of(axis_at):
        return (jnp.arange(array.shape[axis_at]) // (array.shape[axis_at] // blocks)).reshape((-1,) + (1,) * (array.ndim - 1 - axis_at))

    near = jax.random.permutation(stream_key, blocks)[block_of(target)]
    other_side = (block_of(target) + blocks // 2) % blocks
    return jnp.where((block_of(source) == near) | (block_of(source) == other_side), factor * array, array)


def levels(rng, dims, cuts, least, high):
    gain, own = 1.0, jax.random.fold_in(rng, 6)
    for axis_at, blocks in cuts:
        draws = jnp.exp(jax.random.uniform(jax.random.fold_in(own, axis_at), (blocks,), jnp.float32, least / len(cuts), high / len(cuts)))
        gain = gain * jnp.repeat(draws, dims[axis_at] // blocks).reshape([-1 if axis == axis_at else 1 for axis in range(len(dims))])
    return gain


def normal_values(rng, shape, width, reach, shards=(), held_as=jnp.bfloat16):
    result = width * jax.random.normal(rng, shape, jnp.float32)
    if shards:
        result = result * levels(rng, shape, shards, -0.22, 0.18)
    return jnp.clip(result, -reach, reach).astype(held_as)


def heavy_noise(key, dims, deviation, reach, pieces, heavy, held_as=jnp.bfloat16):
    array = deviation * jax.random.normal(key, dims, jnp.float32)
    if pieces:
        array = array * levels(key, dims, pieces, -0.22, 0.18)
    return jnp.clip(raised(array, jax.random.fold_in(key, 3), *heavy), -reach, reach).astype(held_as)


def setup_inputs(seed: int = 0) -> dict:
    arg_keys = jax.random.split(jax.random.key(seed), 4)
    return {
        "grad_parts": heavy_noise(arg_keys[0], (N_REP, EXPERTS, D, FF), 0.5, 3.0, ((0, 4), (2, 16), (3, 4)), (0, 1, 4, 2.0)),
        "momentum": draw_momentum(jax.random.fold_in(arg_keys[3], 71), 0),
        "basis": normal_values(arg_keys[2], (EXPERTS, FF, RANK), FF ** -0.5, 0.15625, ((0, 4), (1, 4))),
    }


def one_expert(grad_parts, momentum, basis, expert):
    parts = lax.dynamic_index_in_dim(grad_parts, expert, 1, keepdims=False)
    gradient = lax.optimization_barrier(jnp.sum(parts.astype(jnp.float32), axis=0))
    buffer = lax.dynamic_index_in_dim(momentum, expert, 0, keepdims=False).astype(jnp.float32) + gradient
    buffer_bf = buffer.astype(jnp.bfloat16)
    left = lax.dynamic_index_in_dim(basis, expert, 0, keepdims=False)
    power = jnp.dot(buffer_bf.astype(jnp.float32), left.astype(jnp.float32), preferred_element_type=jnp.float32)
    gramian = jnp.dot(power.T, power, precision=lax.Precision.HIGHEST)
    factor = jnp.linalg.cholesky(gramian)
    ortho = lax.linalg.triangular_solve(factor, power, left_side=False, lower=True, transpose_a=True)
    ortho_bf = ortho.astype(jnp.bfloat16)
    right = jnp.dot(buffer_bf.T.astype(jnp.float32), ortho_bf.astype(jnp.float32), preferred_element_type=jnp.float32)
    squares = lax.optimization_barrier(jnp.sum(right * right, axis=0))
    basis_next = (right * lax.rsqrt(squares + 1e-06)).astype(jnp.bfloat16)
    right_bf = right.astype(jnp.bfloat16)
    momentum_next = (buffer - 0.05 * jnp.dot(ortho_bf.astype(jnp.float32), right_bf.T.astype(jnp.float32), preferred_element_type=jnp.float32)).astype(jnp.bfloat16)
    scale_factor = (D * FF / RANK) ** 0.5
    update = (scale_factor * jnp.dot(ortho_bf.astype(jnp.float32), basis_next.T.astype(jnp.float32), preferred_element_type=jnp.float32)).astype(jnp.bfloat16)
    return (momentum_next, basis_next, update)

def reference(grad_parts, momentum, basis):

    def run(expert):
        return one_expert(grad_parts, momentum, basis, expert)
    momentum_next, basis_next, update = lax.map(run, jnp.arange(EXPERTS, dtype=jnp.int32))
    return (momentum_next, basis_next, update)
```

```python
import jax
import jax.numpy as jnp
from jax import lax
from jax.experimental import pallas as pl
from jax.experimental.pallas import tpu as pltpu
from jax.sharding import PartitionSpec as P

D = 4096
FF = 1536
RANK = 256
NF = 16
BF = jnp.bfloat16
F32 = jnp.float32
HI = lax.Precision.HIGHEST
MESH = pl.DeviceIdType.MESH
VLIM = 50 * 1024 * 1024


def remote(src, dst, ssem, rsem, **dev):
    return pltpu.make_async_remote_copy(
        src_ref=src, dst_ref=dst, send_sem=ssem, recv_sem=rsem, device_id=dev, device_id_type=MESH
    )


def greet(peers):
    barrier = pltpu.get_barrier_semaphore()
    for dev in peers:
        pl.semaphore_signal(barrier, inc=1, device_id=dev, device_id_type=MESH)
    return barrier


def power_kernel(
    grad, mom, basis,
    buf_out, pow_out, gram_out,
    own, to_r, to_l, rel_a, rel_b, dir_a, dir_b, sum_a, sum_b,
    part, sib, cross, gsend, grecv, gsum, gall,
    load_sem, s_sem, r_sem, b_ssem, b_rsem, x_ssem, x_rsem, g_ssem, g_rsem, h_ssem, h_rsem,
):
    r = lax.axis_index("rep")
    f = lax.axis_index("fsdp")
    t = lax.axis_index("tp")
    xl, core = t // 2, t % 2
    right, left, across = (r + 1) % 4, (r + 3) % 4, (r + 2) % 4
    sibling = xl * 2 + (1 - core)
    partner = (1 - xl) * 2 + core

    loads = [
        pltpu.make_async_copy(grad.at[pl.ds(right * 8, 4)], to_r, load_sem.at[0]),
        pltpu.make_async_copy(grad.at[pl.ds(left * 8 + 4, 4)], to_l, load_sem.at[1]),
        pltpu.make_async_copy(grad.at[pl.ds(r * 8, 8)], own, load_sem.at[2]),
    ]
    for load in loads:
        load.start()

    barrier = greet([{"rep": right}, {"rep": left}, {"tp": sibling}, {"tp": partner}])

    def hello(d, c):
        pl.semaphore_signal(barrier, inc=1, device_id={"fsdp": (f + d) % NF}, device_id_type=MESH)
        return c

    lax.fori_loop(1, NF, hello, 0)
    pl.semaphore_wait(barrier, 4 + NF - 1)

    def relay(k):
        return [
            remote(grad.at[across * 8 + k], rel_a.at[k], s_sem.at[0, k], r_sem.at[0, k], rep=right),
            remote(grad.at[across * 8 + 4 + k], rel_b.at[k], s_sem.at[1, k], r_sem.at[1, k], rep=left),
        ]

    def direct(k):
        return [
            remote(grad.at[right * 8 + 4 + k], dir_b.at[k], s_sem.at[2, k], r_sem.at[2, k], rep=right),
            remote(grad.at[left * 8 + k], dir_a.at[k], s_sem.at[3, k], r_sem.at[3, k], rep=left),
        ]

    def summed(k):
        return [
            remote(to_r.at[k], sum_a.at[k], s_sem.at[4, k], r_sem.at[4, k], rep=right),
            remote(to_l.at[k], sum_b.at[k], s_sem.at[5, k], r_sem.at[5, k], rep=left),
        ]

    def start(copies):
        for copy in copies:
            copy.start()

    def forward(k):
        ra, rb = relay(k)
        sa, sb = summed(k)
        ra.wait_recv()
        to_r[k] = (to_r[k].astype(F32) + rel_a[k].astype(F32)).astype(BF)
        sa.start()
        rb.wait_recv()
        to_l[k] = (to_l[k].astype(F32) + rel_b[k].astype(F32)).astype(BF)
        sb.start()

    def to_sibling(k):
        return remote(part.at[k], sib.at[k // 2], b_ssem.at[k], b_rsem.at[k // 2], tp=sibling)

    def to_partner(k):
        return remote(part.at[k], cross, x_ssem, x_rsem, tp=partner)

    def expert(k, side):
        e = k + 4 * side
        s, d = (sum_a, dir_a) if side == 0 else (sum_b, dir_b)
        total = own[e].astype(F32) + s[k].astype(F32) + d[k].astype(F32)
        held = (mom[e].astype(F32) + total).astype(BF)
        buf_out[e] = held
        part[k, side] = jnp.dot(held, basis[e], preferred_element_type=F32)

    def finish(k):
        sa, sb = summed(k)
        db, da = direct(k)
        sa.wait_recv()
        da.wait_recv()
        expert(k, 0)
        sb.wait_recv()
        db.wait_recv()
        expert(k, 1)

        @pl.when(core != k % 2)
        def _():
            to_sibling(k).start()

    def combine(k):
        @pl.when(core == k % 2)
        def _():
            to_sibling(k).wait_recv()
            part[k] = part[k] + sib[k // 2]

            @pl.when(xl != k // 2)
            def _():
                to_partner(k).start()

    start(relay(0))
    start(relay(1))
    start(direct(0))
    loads[0].wait()
    loads[1].wait()
    forward(0)
    start(relay(2))
    start(direct(1))
    loads[2].wait()
    forward(1)
    start(relay(3))
    start(direct(2))
    finish(0)
    forward(2)
    combine(0)
    start(direct(3))
    finish(1)
    forward(3)
    combine(1)
    finish(2)
    combine(2)
    finish(3)
    combine(3)

    to_partner(0).wait_recv()
    for k in range(4):

        @pl.when(t == k)
        def _():
            pow_out[...] = part[k] + cross[...]

    for i in range(2):
        p = pow_out[i]
        g = lax.dot_general(p, p, (((0,), (0,)), ((), ())), precision=HI, preferred_element_type=F32)
        gsend[:, i] = g.reshape(NF, 16, RANK)
    grecv[f] = gsend[f]

    def scatter(d):
        to, frm = (f + d) % NF, (f + NF - d) % NF
        return (
            remote(gsend.at[to], grecv.at[f], g_ssem.at[d], g_rsem.at[d], fsdp=to),
            remote(gsend.at[to], grecv.at[frm], g_ssem.at[d], g_rsem.at[d], fsdp=to),
        )

    def gather(d):
        to, frm = (f + d) % NF, (f + NF - d) % NF
        return (
            remote(gsum, gall.at[f], h_ssem.at[d], h_rsem.at[d], fsdp=to),
            remote(gsum, gall.at[frm], h_ssem.at[d], h_rsem.at[d], fsdp=to),
        )

    def each(body):
        def step(d, c):
            body(d)
            return c

        lax.fori_loop(1, NF, step, 0)

    each(lambda d: scatter(d)[0].start())
    each(lambda d: scatter(d)[1].wait_recv())
    gsum[...] = jnp.sum(grecv[...], axis=0)
    each(lambda d: gather(d)[0].start())
    gall[f] = gsum[...]
    each(lambda d: gather(d)[1].wait_recv())
    for i in range(2):
        gram_out[i] = gall[:, i].reshape(RANK, RANK)

    each(lambda d: scatter(d)[0].wait_send())
    each(lambda d: gather(d)[0].wait_send())
    for k in range(4):
        for copy in relay(k) + direct(k) + summed(k):
            copy.wait_send()

        @pl.when(core != k % 2)
        def _():
            to_sibling(k).wait_send()

        @pl.when((core == k % 2) & (xl != k // 2))
        def _():
            to_partner(k).wait_send()


def power_call(grad, momentum, basis):
    chunk = (4, 256, 384)
    sem = pltpu.SemaphoreType.DMA
    vm = pl.BlockSpec(memory_space=pltpu.VMEM)
    return pl.pallas_call(
        power_kernel,
        out_shape=(
            jax.ShapeDtypeStruct((8, 256, 384), BF),
            jax.ShapeDtypeStruct((2, RANK, RANK), F32),
            jax.ShapeDtypeStruct((2, RANK, RANK), F32),
        ),
        in_specs=[pl.BlockSpec(memory_space=pl.ANY), vm, vm],
        out_specs=(vm, vm, vm),
        scratch_shapes=[pltpu.VMEM((8, 256, 384), BF)]
        + [pltpu.VMEM(chunk, BF)] * 8
        + [
            pltpu.VMEM((4, 2, 256, 256), F32),
            pltpu.VMEM((2, 2, 256, 256), F32),
            pltpu.VMEM((2, 256, 256), F32),
            pltpu.VMEM((NF, 2, 16, 256), F32),
            pltpu.VMEM((NF, 2, 16, 256), F32),
            pltpu.VMEM((2, 16, 256), F32),
            pltpu.VMEM((NF, 2, 16, 256), F32),
            sem((3,)), sem((6, 4)), sem((6, 4)), sem((4,)), sem((2,)), sem, sem,
            sem((NF,)), sem((NF,)), sem((NF,)), sem((NF,)),
        ],
        compiler_params=pltpu.CompilerParams(
            collective_id=0, has_side_effects=True, vmem_limit_bytes=VLIM
        ),
        name="power",
    )(grad, momentum, basis)


NB = 64


def factor_kernel(gram, power, ortho, work):
    def iota(shape, axis):
        return lax.broadcasted_iota(jnp.int32, shape, axis)

    eye = (iota((RANK, RANK), 0) == iota((RANK, RANK), 1)).astype(F32)
    small = (iota((NB, NB), 0) == iota((NB, NB), 1)).astype(F32)
    sub = iota((8, 128), 0)
    for i in range(2):
        work[i, :, :RANK] = gram[i]
        work[i, :, RANK:] = eye
    for b in range(RANK // NB):
        lo, hi = NB * b, NB * (b + 1)
        rows = []
        for i in range(2):
            m = jnp.concatenate([work[i, lo:hi, lo:hi], small], axis=1)
            rows.append([m[8 * q : 8 * q + 8] for q in range(NB // 8)])
        for q0 in range(NB // 8):
            diag = [None, None]
            for jj in range(8):
                j = 8 * q0 + jj
                for i in range(2):
                    m = rows[i]
                    cols = [jnp.broadcast_to(m[q][:, j : j + 1], (8, 128)) for q in range(q0, NB // 8)]
                    scaled = m[q0][jj : jj + 1] / cols[0][jj : jj + 1]
                    diag[i] = cols[0] if jj == 0 else jnp.where(sub == jj, cols[0], diag[i])
                    m[q0] = m[q0] - jnp.where(sub > jj, cols[0], 0.0) * scaled
                    for q in range(q0 + 1, NB // 8):
                        m[q] = m[q] - cols[q - q0] * scaled
            for i in range(2):
                rows[i][q0] = rows[i][q0] * lax.rsqrt(diag[i])
        for i in range(2):
            inv = jnp.concatenate(rows[i], axis=0)[:, NB:]
            a, z = hi // 128 * 128, -(-(RANK + hi) // 128) * 128
            x = jnp.dot(inv, work[i, lo:hi, a:z], precision=HI, preferred_element_type=F32)
            work[i, lo:hi, a:z] = x
            if hi < RANK:
                panel = x[:, hi - a : RANK - a]
                work[i, hi:, a:z] = work[i, hi:, a:z] - lax.dot_general(
                    panel, x, (((0,), (0,)), ((), ())), precision=HI, preferred_element_type=F32
                )
    for i in range(2):
        ortho[i] = lax.dot_general(
            power[i], work[i, :, RANK:], (((1,), (1,)), ((), ())), precision=HI, preferred_element_type=F32
        ).astype(BF)


def factor_call(gram, power):
    vm = pl.BlockSpec(memory_space=pltpu.VMEM)
    return pl.pallas_call(
        factor_kernel,
        out_shape=jax.ShapeDtypeStruct((2, 256, RANK), BF),
        in_specs=[vm, vm],
        out_specs=vm,
        scratch_shapes=[pltpu.VMEM((2, RANK, 2 * RANK), F32)],
        compiler_params=pltpu.CompilerParams(vmem_limit_bytes=VLIM),
        name="factor",
    )(gram, power)


def right_kernel(
    ortho, buf,
    ortho_all, right_all, squares,
    acc, flow, swap_to, swap_from, sq_mine, sq_recv,
    o_ssem, o_rsem, f_ssem, f_rsem, w_ssem, w_rsem, a_ssem, a_rsem, q_ssem, q_rsem,
):
    f = lax.axis_index("fsdp")
    t = lax.axis_index("tp")
    xl, core = t // 2, t % 2
    sibling = xl * 2 + (1 - core)
    partner = (1 - xl) * 2 + core
    diagonal = (1 - xl) * 2 + (1 - core)
    z, xh = f // 2, f % 2
    up, down = ((z + 1) % 8) * 2 + xh, ((z + 7) % 8) * 2 + xh
    other = z * 2 + (1 - xh)

    barrier = greet(
        [{"tp": sibling}, {"tp": partner}, {"tp": diagonal}, {"fsdp": up}, {"fsdp": down}, {"fsdp": other}]
    )
    ortho_all[t] = ortho[...]
    pl.semaphore_wait(barrier, 6)

    near = remote(ortho_all.at[t], ortho_all.at[t], o_ssem.at[0], o_rsem.at[0], tp=sibling)
    far = remote(ortho_all.at[t], ortho_all.at[t], o_ssem.at[1], o_rsem.at[1], tp=partner)
    passed = remote(ortho_all.at[partner], ortho_all.at[partner], o_ssem.at[2], o_rsem.at[2], tp=sibling)
    near_in = remote(ortho_all.at[sibling], ortho_all.at[sibling], o_ssem.at[0], o_rsem.at[0], tp=sibling)
    far_in = remote(ortho_all.at[partner], ortho_all.at[partner], o_ssem.at[1], o_rsem.at[1], tp=partner)
    passed_in = remote(ortho_all.at[diagonal], ortho_all.at[diagonal], o_ssem.at[2], o_rsem.at[2], tp=sibling)
    far.start()
    near.start()

    def product(owner):
        for side in range(2):
            acc[owner + 4 * side] = lax.dot_general(
                buf[owner + 4 * side], ortho_all[owner, side],
                (((0,), (0,)), ((), ())), preferred_element_type=F32,
            ).astype(BF)

    product(t)
    near_in.wait_recv()
    product(sibling)
    far_in.wait_recv()
    passed.start()
    product(partner)
    passed_in.wait_recv()
    product(diagonal)

    def half(ref, at, h):
        return ref.at[at, pl.ds(192 * h, 192)]

    def hop(way, left, h):
        target = (z + left) % 8 if way == 0 else (z + 8 - left) % 8
        return remote(
            half(acc, target, h), flow.at[way, left - 1, h],
            f_ssem.at[way, left - 1, h], f_rsem.at[way, left - 1, h],
            fsdp=up if way == 0 else down,
        )

    def long(way):
        return way

    hop(0, 4, long(0)).start()
    hop(1, 4, long(1)).start()
    hop(0, 3, 1 - long(0)).start()
    hop(1, 3, 1 - long(1)).start()
    for left in (4, 3, 2):
        for way in range(2):
            halves = (long(way),) if left == 4 else (long(way), 1 - long(way))
            for h in halves:
                hop(way, left, h).wait_recv()
                target = (z + left - 1) % 8 if way == 0 else (z + 9 - left) % 8
                at = pl.ds(192 * h, 192)
                acc[target, at] = (
                    acc[target, at].astype(F32) + flow[way, left - 1, h].astype(F32)
                ).astype(BF)
                hop(way, left - 1, h).start()
    swap = remote(swap_to, swap_from, w_ssem, w_rsem, fsdp=other)
    for h in range(2):
        for way in range(2):
            hop(way, 1, h).wait_recv()
        at = pl.ds(192 * h, 192)
        swap_to[at] = (
            acc[z, at].astype(F32) + flow[0, 0, h].astype(F32) + flow[1, 0, h].astype(F32)
        ).astype(BF)
    swap.start()
    swap.wait_recv()
    right_all[z] = (swap_to[...].astype(F32) + swap_from[...].astype(F32)).astype(BF)

    def spread(way, gone, h):
        source = (z + 8 - gone) % 8 if way == 0 else (z + gone) % 8
        return remote(
            half(right_all, source, h), half(right_all, source, h),
            a_ssem.at[way, gone, h], a_rsem.at[way, gone, h],
            fsdp=up if way == 0 else down,
        )

    def arrived(way, gone, h):
        source = (z + 7 - gone) % 8 if way == 0 else (z + gone + 1) % 8
        return remote(
            half(right_all, source, h), half(right_all, source, h),
            a_ssem.at[way, gone, h], a_rsem.at[way, gone, h],
            fsdp=up if way == 0 else down,
        )

    for h in range(2):
        for way in range(2):
            spread(way, 0, h).start()
    for gone in range(4):
        for way in range(2):
            halves = (long(way), 1 - long(way)) if gone < 3 else (long(way),)
            for h in halves:
                arrived(way, gone, h).wait_recv()
                if gone + 1 < (4 if h == long(way) else 3):
                    spread(way, gone + 1, h).start()

    for e in range(8):
        full = right_all[e].astype(F32)
        sq_mine[e : e + 1] = jnp.sum(full * full, axis=0, keepdims=True)

    def tell(n, dev):
        return remote(sq_mine, sq_recv.at[n], q_ssem.at[n], q_rsem.at[n], tp=dev)

    tells = [tell(0, sibling), tell(1, partner), tell(2, diagonal)]
    for copy in tells:
        copy.start()
    for copy in tells:
        copy.wait_recv()
    squares[...] = (sq_mine[...] + sq_recv[0]) + (sq_recv[1] + sq_recv[2])

    near.wait_send()
    far.wait_send()
    passed.wait_send()
    swap.wait_send()
    for copy in tells:
        copy.wait_send()
    for way in range(2):
        for h in range(2):
            for n in range(4 if h == long(way) else 3):
                hop(way, n + 1, h).wait_send()
                spread(way, n, h).wait_send()


def right_call(ortho, buf):
    sem = pltpu.SemaphoreType.DMA
    vm = pl.BlockSpec(memory_space=pltpu.VMEM)
    return pl.pallas_call(
        right_kernel,
        out_shape=(
            jax.ShapeDtypeStruct((4, 2, 256, RANK), BF),
            jax.ShapeDtypeStruct((8, 384, RANK), BF),
            jax.ShapeDtypeStruct((8, RANK), F32),
        ),
        in_specs=[vm, vm],
        out_specs=(vm, vm, vm),
        scratch_shapes=[
            pltpu.VMEM((8, 384, RANK), BF),
            pltpu.VMEM((2, 4, 2, 192, RANK), BF),
            pltpu.VMEM((384, RANK), BF),
            pltpu.VMEM((384, RANK), BF),
            pltpu.VMEM((8, RANK), F32),
            pltpu.VMEM((3, 8, RANK), F32),
            sem((3,)), sem((3,)), sem((2, 4, 2)), sem((2, 4, 2)), sem, sem,
            sem((2, 4, 2)), sem((2, 4, 2)), sem((3,)), sem((3,)),
        ],
        compiler_params=pltpu.CompilerParams(
            collective_id=1, has_side_effects=True, vmem_limit_bytes=VLIM
        ),
        name="right",
    )(ortho, buf)


def output_kernel(buf, ortho, right, squares, mom_next, basis_next, update):
    e = pl.program_id(0)
    r = right[0]
    scale = lax.rsqrt(squares[pl.ds(e, 1)] + 1e-06)
    nxt = (r.astype(F32) * scale).astype(BF)
    basis_next[0] = nxt
    o = ortho[0, 0]
    dims = (((1,), (1,)), ((), ()))
    back = lax.dot_general(o, r, dims, preferred_element_type=F32)
    mom_next[0] = (buf[0].astype(F32) - 0.05 * back).astype(BF)
    up = lax.dot_general(o, nxt, dims, preferred_element_type=F32)
    update[0] = ((D * FF / RANK) ** 0.5 * up).astype(BF)


def output_call(buf, ortho, right, squares):
    wide = pl.BlockSpec((1, 256, 384), lambda e: (e, 0, 0))
    tall = pl.BlockSpec((1, 384, RANK), lambda e: (e, 0, 0))
    return pl.pallas_call(
        output_kernel,
        grid=(8,),
        out_shape=(
            jax.ShapeDtypeStruct((8, 256, 384), BF),
            jax.ShapeDtypeStruct((8, 384, RANK), BF),
            jax.ShapeDtypeStruct((8, 256, 384), BF),
        ),
        in_specs=[
            wide,
            pl.BlockSpec((1, 1, 256, RANK), lambda e: (e % 4, e // 4, 0, 0)),
            tall,
            pl.BlockSpec((8, RANK), lambda e: (0, 0)),
        ],
        out_specs=(wide, tall, wide),
        compiler_params=pltpu.CompilerParams(vmem_limit_bytes=VLIM),
        name="outputs",
    )(buf, ortho, right, squares)


def on_device(grad_parts, momentum, basis):
    buf, power, gram = power_call(grad_parts[0], momentum, basis)
    ortho = factor_call(gram, power)
    ortho_all, right, squares = right_call(ortho, buf)
    return output_call(buf, ortho_all, right, squares)


def solution(mesh):
    placed = (P("rep", None, "fsdp", "tp"), P("rep", "fsdp", "tp"), P("rep", "tp", None))
    return jax.shard_map(
        on_device,
        mesh=mesh,
        in_specs=placed,
        out_specs=(P("rep", "fsdp", "tp"), P("rep", "tp", None), P("rep", "fsdp", "tp")),
        check_vma=False,
    )
```
